128 devices in a mesh: row: 8 (over z, core), col: 16 (over y, x).
Axes of the slice: x: 4, y: 4, z: 4, core: 2. Of those that a mesh axis runs over, the one named last changes fastest.
Arguments:
- density_blocks: bfloat16 [1024, 16, 128, 128], P(('row', 'col')), may hold values from -6 to 6
- hamilton_blocks: bfloat16 [1024, 16, 128, 128], P(('row', 'col')), may hold values from -0.25 to 0.25
- density_cols: int32 [1024, 16], replicated, may hold values from 0 to 1023, as said below
- hamilton_cols: int32 [1024, 16], replicated, may hold values from 0 to 1023, as said below
Outputs:
- product_blocks: bfloat16 [1024, 16, 128, 128], P(('row', 'col'))
The draws below stay inside these ranges and needn't reach their ends.
Inputs may be any that keep to these rules, and one draw needn't show every extreme that they name: `density_cols`: row r lists 16 distinct block columns in increasing order, each within 24 of r, r itself among them. `hamilton_cols`: row r lists 16 distinct block columns in increasing order, each within 24 of r, r itself among them.
All inputs are finite; a program needn't handle non-finite values.
Results may differ from the reference program's by a relative error of at most 0.001.
Values may be sent and summed in bfloat16 or wider, within the bound.
A program may use at most 192 MiB of HBM per device.

```python
import jax
import jax.numpy as jnp
from jax import lax

B = 128
W = 24
LIST = 16
RDEV = 8
COLS = 16
NB = 1024


def banded_lists(key):
    row_ids = jnp.arange(NB, dtype=jnp.int32)[:, None]
    offsets = jnp.arange(2 * W + 1, dtype=jnp.int32)[None, :]
    columns = row_ids - W + offsets
    allowed = (columns >= 0) & (columns < NB) & (columns != row_ids)
    scores = jax.random.randint(key, (NB, 2 * W + 1), 0, 1 << 20, dtype=jnp.int32) * (2 * W + 1) + offsets
    scores = jnp.where(allowed, scores, -1)
    top_scores, chosen = lax.top_k(scores, LIST - 1)
    picked = jnp.take_along_axis(columns, chosen, axis=1)
    listed = jnp.concatenate([picked, row_ids], axis=1)
    return jnp.sort(listed, axis=1).astype(jnp.int32)


def draw_density_cols(key, part):
    key = jax.random.fold_in(key, 11)
    return banded_lists(key)


def draw_hamilton_cols(key, part):
    key = jax.random.fold_in(key, 23)
    return banded_lists(key)


def level_of(own_key, extent, split, low, largest):
    gain, own = 1.0, jax.random.fold_in(own_key, 6)
    for axis_at, parts in split:
        steps = jnp.exp(jax.random.uniform(jax.random.fold_in(own, axis_at), (parts,), jnp.float32, low / len(split), largest / len(split)))
        gain = gain * jnp.repeat(steps, extent[axis_at] // parts).reshape([-1 if axis == axis_at else 1 for axis in range(len(extent))])
    return gain


def noise(key, shape, deviation, limit, pieces=(), kind=jnp.bfloat16):
    level = level_of(key, shape, pieces, -0.22, 0.18) if pieces else 1.0
    entries = jax.random.normal(key, shape, jnp.float32) * deviation * level
    return jnp.minimum(jnp.maximum(entries, -limit), limit).astype(kind)


def setup_inputs(seed: int = 0) -> dict:
    seeds = jax.random.split(jax.random.key(seed), 5)
    return {
        "density_blocks": noise(seeds[0], (NB, LIST, B, B), 1.0, 6.0, ((0, 128),)),
        "hamilton_blocks": noise(seeds[1], (NB, LIST, B, B), (4 * B) ** -0.5, 0.25, ((0, 128),)),
        "density_cols": draw_density_cols(jax.random.fold_in(seeds[4], 71), 0),
        "hamilton_cols": draw_hamilton_cols(jax.random.fold_in(seeds[4], 71), 0),
    }


def storage_slot(block_row):
    upper = block_row // (COLS * RDEV)
    middle = (block_row // RDEV) % COLS
    lower = block_row % RDEV
    return ((lower * COLS + middle) * RDEV + upper).astype(jnp.int32)


def reference(density_blocks, hamilton_blocks, density_cols, hamilton_cols):
    def one_slot(slot):
        block_row = storage_slot(slot)
        left_list = jnp.take(density_cols, block_row, axis=0)
        left_row = jnp.take(density_blocks, slot, axis=0).astype(jnp.float32)
        right_rows = jnp.take(hamilton_blocks, storage_slot(left_list), axis=0).astype(jnp.float32)
        right_lists = jnp.take(hamilton_cols, left_list, axis=0)
        matches = (right_lists[None, :, :] == left_list[:, None, None]).astype(jnp.float32)
        collected = jnp.einsum("qmn,mnbc->qmbc", matches, right_rows, precision=lax.Precision.HIGHEST)
        summed = jnp.einsum("mab,qmbc->qac", left_row, collected, precision=lax.Precision.HIGHEST)
        return summed.astype(jnp.bfloat16)

    slots = jnp.arange(NB, dtype=jnp.int32)
    return lax.map(one_slot, slots)
```

```python
import functools

import jax
import jax.numpy as jnp
from jax import lax
from jax.experimental import pallas as pl
from jax.experimental.pallas import tpu as pltpu
from jax.sharding import PartitionSpec as P

W = 24
LIST = 16
ROWS = 8
WINDOW = 2 * W + ROWS
MESH = pl.DeviceIdType.MESH
OWN, SIB, PAIR, PAIRF, YA, YB, YBF, DIN, OUT = range(9)


class Place:
    def __init__(self):
        self.row = lax.axis_index("row")
        self.col = lax.axis_index("col")
        self.z, self.core = self.row // 2, self.row % 2
        self.y, self.x = self.col // 4, self.col % 4
        self.half = self.x // 2
        self.side = (self.x + self.half) % 2
        self.slot = self.side * 4 + self.z
        self.group = self.slot * 4 + self.y
        self.quarter = self.half * 2 + self.core
        self.start = self.group * 32 + self.quarter * 8

    def home(self, slot):
        side = slot // 4
        x = side + self.half * (3 - 2 * side)
        return ((slot % 4) * 2 + self.x % 2, self.y * 4 + x)

    def source(self, k):
        return (k, self.y * 4 + self.quarter)

    def member(self, group, core):
        slot = group // 4
        side = slot // 4
        x = side + self.half * (3 - 2 * side)
        return ((slot % 4) * 2 + core, (group % 4) * 4 + x)


def kernel(index_ref, d_ref, h_ref, out_ref, window, dbuf, obuf, send, recv):
    at = Place()
    row, core = at.row, at.core
    sibling = (at.row + 1 - 2 * core, at.col)
    pair = (at.row, at.y * 4 + 3 - at.x)
    heading = 1 - 2 * at.half
    facing = 2 * core - 1
    across = at.group + facing
    ahead = at.group + heading
    behind = at.group - heading
    has_across = (across >= 0) & (across < 32)
    has_ahead = (ahead >= 0) & (ahead < 32)
    has_behind = (behind >= 0) & (behind < 32)
    across_dev = at.member(across, 1 - core)
    ahead_dev = at.member(ahead, core)
    behind_dev = at.member(behind, core)
    stays = at.x % 2 == core

    barrier = pltpu.get_barrier_semaphore()

    def greet(dev):
        pl.semaphore_signal(barrier, inc=1, device_id=dev, device_id_type=MESH)

    def greet_slot(i, _):
        @pl.when(jnp.logical_not(stays & (i == at.slot)))
        def _():
            greet(at.home(i))

        @pl.when(jnp.logical_not(stays & (i == row)))
        def _():
            greet(at.source(i))

        return 0

    lax.fori_loop(0, 8, greet_slot, 0)
    greet(sibling)
    greet(pair)
    pl.when(has_across)(lambda: greet(across_dev))
    pl.when(has_ahead)(lambda: greet(ahead_dev))
    pl.when(has_behind)(lambda: greet(behind_dev))
    count = (
        18
        - 2 * stays.astype(jnp.int32)
        + has_across.astype(jnp.int32)
        + has_ahead.astype(jnp.int32)
        + has_behind.astype(jnp.int32)
    )
    pl.semaphore_wait(barrier, count)

    def rows(w):
        return window.at[pl.ds(w * LIST, LIST)]

    def remote(src, dst, kind, s, r, dev):
        return pltpu.make_async_remote_copy(
            src_ref=src,
            dst_ref=dst,
            send_sem=send.at[kind, s],
            recv_sem=recv.at[kind, r],
            device_id=dev,
            device_id_type=MESH,
        )

    own = W
    to_sib = own + 8 * facing
    at_pair = own + 16 * heading
    to_pair = own - 16 * heading
    pair_to_sib = own + 16 * heading + 8 * facing
    to_across = own - 24 * facing
    at_ahead = own - 16 * heading
    behind_to_sib = own - 16 * heading + 8 * facing

    def send_in(src_ref, dst, kind):
        def body(i, _):
            slot = (i + row) % 8
            local = stays & (slot == at.slot)

            @pl.when(local)
            def _():
                pltpu.make_async_copy(src_ref.at[slot], dst, recv.at[kind, row]).start()

            @pl.when(jnp.logical_not(local))
            def _():
                remote(src_ref.at[slot], dst, kind, slot, row, at.home(slot)).start()

            return 0

        lax.fori_loop(0, 8, body, 0)

    send_in(h_ref, rows(own + row), OWN)
    send_in(d_ref, dbuf.at[pl.ds(row * LIST, LIST)], DIN)

    def arrived(ref, kind, k):
        pltpu.make_async_copy(ref, ref, recv.at[kind, k]).wait()

    def step(j, _):
        @pl.when(j < 8)
        def _():
            k = (at.slot - j + 8) % 8
            here = rows(own + k)
            arrived(here, OWN, k)
            remote(here, rows(to_pair + k), PAIR, k, k, pair).start()

            @pl.when(has_across)
            def _():
                remote(here, rows(to_across + k), YA, k, k, across_dev).start()

            remote(here, rows(to_sib + k), SIB, k, k, sibling).start()

        @pl.when(j >= 1)
        def _():
            k = (at.slot - j + 9) % 8
            here = rows(at_pair + k)
            arrived(here, PAIR, k)

            @pl.when(has_ahead)
            def _():
                remote(here, rows(at_ahead + k), YB, k, k, ahead_dev).start()

            remote(here, rows(pair_to_sib + k), PAIRF, k, k, sibling).start()

        return 0

    lax.fori_loop(0, 9, step, 0)

    def hand_on(j, _):
        k = (at.slot - j + 8) % 8
        here = rows(at_ahead + k)
        arrived(here, YB, k)
        remote(here, rows(behind_to_sib + k), YBF, k, k, sibling).start()
        return 0

    @pl.when(has_behind)
    def _():
        lax.fori_loop(0, 8, hand_on, 0)

    zero = WINDOW * LIST
    window[zero] = jnp.zeros(window.shape[1:], window.dtype)

    def collect(k, _):
        one = rows(k)
        arrived(one, SIB, k)
        arrived(one, PAIRF, k)

        @pl.when(has_across)
        def _():
            arrived(one, YA, k)

        @pl.when(has_behind)
        def _():
            arrived(one, YBF, k)

        arrived(one, DIN, k)
        return 0

    lax.fori_loop(0, 8, collect, 0)

    def multiply(j, _):
        k = (row + j) % 8

        def columns(p, _):
            total = jnp.zeros((128, 256), jnp.float32)
            for m in range(0, LIST, 2):
                left = jnp.concatenate([dbuf[k * LIST + m], dbuf[k * LIST + m + 1]], axis=1)
                base = (k * LIST + m) * LIST + 2 * p
                upper = jnp.concatenate([window[index_ref[base]], window[index_ref[base + 1]]], axis=1)
                lower = jnp.concatenate(
                    [window[index_ref[base + LIST]], window[index_ref[base + LIST + 1]]], axis=1
                )
                right = jnp.concatenate([upper, lower], axis=0)
                total = total + jnp.dot(left, right, preferred_element_type=jnp.float32)
            obuf[k * LIST + 2 * p] = total[:, :128].astype(obuf.dtype)
            obuf[k * LIST + 2 * p + 1] = total[:, 128:].astype(obuf.dtype)
            return 0

        lax.fori_loop(0, LIST // 2, columns, 0)
        here = obuf.at[pl.ds(k * LIST, LIST)]
        local = stays & (k == row)

        @pl.when(local)
        def _():
            pltpu.make_async_copy(here, out_ref.at[at.slot], recv.at[OUT, at.slot]).start()

        @pl.when(jnp.logical_not(local))
        def _():
            remote(here, out_ref.at[at.slot], OUT, k, at.slot, at.source(k)).start()

        return 0

    lax.fori_loop(0, 8, multiply, 0)

    def finish(k, _):
        one = rows(k)

        def sent(kind):
            pltpu.make_async_copy(one, one, send.at[kind, k]).wait()

        @pl.when(jnp.logical_not(stays & (k == at.slot)))
        def _():
            sent(OWN)
            sent(DIN)

        sent(SIB)
        sent(PAIR)
        sent(PAIRF)
        pl.when(has_across)(lambda: sent(YA))
        pl.when(has_ahead)(lambda: sent(YB))
        pl.when(has_behind)(lambda: sent(YBF))

        @pl.when(jnp.logical_not(stays & (k == row)))
        def _():
            sent(OUT)

        arrived(out_ref.at[k], OUT, k)
        return 0

    lax.fori_loop(0, 8, finish, 0)


def match_index(density_cols, hamilton_cols):
    start = Place().start
    left = lax.dynamic_slice_in_dim(density_cols, start, ROWS, 0)
    right = jnp.take(hamilton_cols, left, axis=0)
    hit = right[:, :, None, :] == left[:, None, :, None]
    n = jnp.arange(LIST, dtype=jnp.int32)
    which = jnp.sum(jnp.where(hit, n, 0), axis=-1)
    block = (left - start + W)[:, :, None] * LIST + which
    return jnp.where(jnp.any(hit, axis=-1), block, WINDOW * LIST).reshape(-1).astype(jnp.int32)


def per_device(density_blocks, hamilton_blocks, density_cols, hamilton_cols):
    index = match_index(density_cols, hamilton_cols)
    block = density_blocks.shape[2:]
    kind = density_blocks.dtype
    return pl.pallas_call(
        kernel,
        out_shape=jax.ShapeDtypeStruct(density_blocks.shape, kind),
        in_specs=[
            pl.BlockSpec(memory_space=pltpu.SMEM),
            pl.BlockSpec(memory_space=pl.ANY),
            pl.BlockSpec(memory_space=pl.ANY),
        ],
        out_specs=pl.BlockSpec(memory_space=pl.ANY),
        scratch_shapes=[
            pltpu.VMEM((WINDOW * LIST + 1, *block), kind),
            pltpu.VMEM((ROWS * LIST, *block), kind),
            pltpu.VMEM((ROWS * LIST, *block), kind),
            pltpu.SemaphoreType.DMA((9, 8)),
            pltpu.SemaphoreType.DMA((9, 8)),
        ],
        compiler_params=pltpu.CompilerParams(
            collective_id=0, has_side_effects=True, vmem_limit_bytes=52 << 20
        ),
        name="block_product",
    )(index, density_blocks, hamilton_blocks)


def solution(mesh):
    return jax.shard_map(
        per_device,
        mesh=mesh,
        in_specs=(
            P(("row", "col"), None, None, None),
            P(("row", "col"), None, None, None),
            P(),
            P(),
        ),
        out_specs=P(("row", "col"), None, None, None),
        check_vma=False,
    )
```

```python
import functools

import jax
import jax.numpy as jnp
from jax import lax
from jax.experimental import pallas as pl
from jax.experimental.pallas import tpu as pltpu
from jax.sharding import PartitionSpec as P

W = 24
LIST = 16
ROWS = 8
WINDOW = 2 * W + ROWS
MESH = pl.DeviceIdType.MESH
OWN, SIB, PAIR, PAIRF, YA, YB, YBF, DIN, OUT, RA, RAF, RB, RBF = range(13)
DETOUR = 2


class Place:
    def __init__(self):
        self.row = lax.axis_index("row")
        self.col = lax.axis_index("col")
        self.z, self.core = self.row // 2, self.row % 2
        self.y, self.x = self.col // 4, self.col % 4
        self.half = self.x // 2
        self.side = (self.x + self.half) % 2
        self.slot = self.side * 4 + self.z
        self.group = self.slot * 4 + self.y
        self.quarter = self.half * 2 + self.core
        self.start = self.group * 32 + self.quarter * 8

    def home(self, slot):
        side = slot // 4
        x = side + self.half * (3 - 2 * side)
        return ((slot % 4) * 2 + self.x % 2, self.y * 4 + x)

    def source(self, k):
        return (k, self.y * 4 + self.quarter)

    def member(self, group, core):
        slot = group // 4
        side = slot // 4
        x = side + self.half * (3 - 2 * side)
        return ((slot % 4) * 2 + core, (group % 4) * 4 + x)


def turn(i):
    i = i // 2
    return i + (i // 2) * (1 - 2 * (i % 2))


def arrival(z, j):
    return ((z - turn(j) + 4) % 4) * 2 + j % 2


def kernel(index_ref, d_ref, h_ref, out_ref, window, dbuf, obuf, rbuf, send, recv):
    at = Place()
    row, core = at.row, at.core
    sibling = (at.row + 1 - 2 * core, at.col)
    pair = (at.row, at.y * 4 + 3 - at.x)
    heading = 1 - 2 * at.half
    facing = 2 * core - 1
    across = at.group + facing
    ahead = at.group + heading
    behind = at.group - heading
    has_across = (across >= 0) & (across < 32)
    has_ahead = (ahead >= 0) & (ahead < 32)
    has_behind = (behind >= 0) & (behind < 32)
    across_dev = at.member(across, 1 - core)
    ahead_dev = at.member(ahead, core)
    behind_dev = at.member(behind, core)
    stays = at.x % 2 == core
    seam_a = has_across & (at.y == 3 * core)
    relay_a = (at.y == 3 - 3 * core) & (at.slot + facing >= 0) & (at.slot + facing < 8)
    a_next = at.member(at.group + 4 * facing, 1 - core)
    a_from = at.member(at.group - 3 * facing, core)
    a_to = at.member(at.group + 3 * facing, core)
    edge = at.y == 3 * (1 - at.half)
    seam_b = has_ahead & edge
    relay_b = edge & (at.slot - heading >= 0) & (at.slot - heading < 8)
    b_next = at.member(at.group + 4 * heading, core)
    b_last = at.member(at.group - 4 * heading, core)
    b_to = at.member(at.group - 3 * heading, core)
    from_b = at.member(at.group + 3 * heading, core)
    seam_in = has_behind & (at.y == 3 * at.half)

    barrier = pltpu.get_barrier_semaphore()

    def greet(dev):
        pl.semaphore_signal(barrier, inc=1, device_id=dev, device_id_type=MESH)

    def greet_slot(i, _):
        @pl.when(jnp.logical_not(stays & (i == at.slot)))
        def _():
            greet(at.home(i))

        @pl.when(jnp.logical_not(stays & (i == row)))
        def _():
            greet(at.source(i))

        return 0

    lax.fori_loop(0, 8, greet_slot, 0)
    greet(sibling)
    greet(pair)
    pl.when(has_across & jnp.logical_not(seam_a))(lambda: greet(across_dev))
    pl.when(seam_a)(lambda: (greet(a_next), greet(a_from)) and None)
    pl.when(relay_a)(lambda: (greet(a_next), greet(a_to)) and None)
    pl.when(seam_b)(lambda: greet(b_next))
    pl.when(seam_in)(lambda: greet(from_b))
    pl.when(relay_b)(lambda: (greet(b_last), greet(b_to)) and None)
    pl.when(has_ahead)(lambda: greet(ahead_dev))
    pl.when(has_behind)(lambda: greet(behind_dev))
    count = (
        18
        - 2 * stays.astype(jnp.int32)
        + has_across.astype(jnp.int32)
        + seam_a.astype(jnp.int32)
        + 2 * relay_a.astype(jnp.int32)
        + seam_b.astype(jnp.int32)
        + seam_in.astype(jnp.int32)
        + 2 * relay_b.astype(jnp.int32)
        + has_ahead.astype(jnp.int32)
        + has_behind.astype(jnp.int32)
    )
    pl.semaphore_wait(barrier, count)

    def rows(w):
        return window.at[pl.ds(w * LIST, LIST)]

    def remote(src, dst, kind, s, r, dev, sent=None):
        return pltpu.make_async_remote_copy(
            src_ref=src,
            dst_ref=dst,
            send_sem=send.at[kind if sent is None else sent, s],
            recv_sem=recv.at[kind, r],
            device_id=dev,
            device_id_type=MESH,
        )

    own = W
    to_sib = own + 8 * facing
    at_pair = own + 16 * heading
    to_pair = own - 16 * heading
    pair_to_sib = own + 16 * heading + 8 * facing
    to_across = own - 24 * facing
    at_ahead = own - 16 * heading
    behind_to_sib = own - 16 * heading + 8 * facing

    def send_in(src_ref, dst, kind):
        def body(i, _):
            slot = (at.side * (1 - 2 * (i % 2)) + i % 2) * 4 + (at.z + turn(i)) % 4
            local = stays & (slot == at.slot)

            @pl.when(local)
            def _():
                pltpu.make_async_copy(src_ref.at[slot], dst, recv.at[kind, row]).start()

            @pl.when(jnp.logical_not(local))
            def _():
                remote(src_ref.at[slot], dst, kind, slot, row, at.home(slot)).start()

            return 0

        lax.fori_loop(0, 8, body, 0)

    send_in(h_ref, rows(own + row), OWN)

    def relayed(i):
        return rbuf.at[pl.ds(i * LIST, LIST)]

    def arrived(ref, kind, k):
        pltpu.make_async_copy(ref, ref, recv.at[kind, k]).wait()

    def step(j, _):
        @pl.when(j < 8)
        def _():
            k = arrival(at.z, j)
            here = rows(own + k)
            arrived(here, OWN, k)
            remote(here, rows(to_pair + k), PAIR, k, k, pair).start()

            @pl.when(has_across & jnp.logical_not(seam_a))
            def _():
                remote(here, rows(to_across + k), YA, k, k, across_dev).start()

            @pl.when(seam_a)
            def _():
                remote(here, relayed(k), RA, k, k, a_next, YA).start()

            remote(here, rows(to_sib + k), SIB, k, k, sibling).start()

        @pl.when(j >= 1)
        def _():
            k = arrival(at.z, j - 1)
            here = rows(at_pair + k)
            arrived(here, PAIR, k)

            around = seam_b & (j - 1 < DETOUR)

            @pl.when(has_ahead & jnp.logical_not(around))
            def _():
                remote(here, rows(at_ahead + k), YB, k, k, ahead_dev).start()

            @pl.when(around)
            def _():
                remote(here, relayed(7 + j), RB, k, k, b_next, YB).start()

            remote(here, rows(pair_to_sib + k), PAIRF, k, k, sibling).start()

        @pl.when((j >= 1) & relay_a)
        def _():
            k = arrival((at.z + facing + 4) % 4, j - 1)
            here = relayed(k)
            arrived(here, RA, k)
            remote(here, rows(own + 24 * facing + k), YA, k, k, a_to, RAF).start()

        @pl.when((j >= 2) & (j < 2 + DETOUR) & relay_b)
        def _():
            k = arrival((at.z - heading + 4) % 4, j - 2)
            here = relayed(6 + j)
            arrived(here, RB, k)
            remote(here, rows(at_ahead + k), YB, k, k, b_to, RBF).start()

        return 0

    lax.fori_loop(0, 9, step, 0)
    send_in(d_ref, dbuf.at[pl.ds(row * LIST, LIST)], DIN)

    def hand_on(j, _):
        k = arrival((behind // 4) % 4, j)
        here = rows(at_ahead + k)
        arrived(here, YB, k)
        remote(here, rows(behind_to_sib + k), YBF, k, k, sibling).start()
        return 0

    @pl.when(has_behind)
    def _():
        lax.fori_loop(0, 8, hand_on, 0)

    zero = WINDOW * LIST
    window[zero] = jnp.zeros(window.shape[1:], window.dtype)

    def collect(k, _):
        one = rows(k)
        arrived(one, SIB, k)
        arrived(one, PAIRF, k)

        @pl.when(has_across)
        def _():
            arrived(one, YA, k)

        @pl.when(has_behind)
        def _():
            arrived(one, YBF, k)

        arrived(one, DIN, k)
        return 0

    lax.fori_loop(0, 8, collect, 0)

    def multiply(j, _):
        k = (row + j) % 8

        def columns(p, _):
            total = jnp.zeros((128, 256), jnp.float32)
            for m in range(0, LIST, 2):
                left = jnp.concatenate([dbuf[k * LIST + m], dbuf[k * LIST + m + 1]], axis=1)
                base = (k * LIST + m) * LIST + 2 * p
                upper = jnp.concatenate([window[index_ref[base]], window[index_ref[base + 1]]], axis=1)
                lower = jnp.concatenate(
                    [window[index_ref[base + LIST]], window[index_ref[base + LIST + 1]]], axis=1
                )
                right = jnp.concatenate([upper, lower], axis=0)
                total = total + jnp.dot(left, right, preferred_element_type=jnp.float32)
            obuf[k * LIST + 2 * p] = total[:, :128].astype(obuf.dtype)
            obuf[k * LIST + 2 * p + 1] = total[:, 128:].astype(obuf.dtype)
            return 0

        lax.fori_loop(0, LIST // 2, columns, 0)
        here = obuf.at[pl.ds(k * LIST, LIST)]
        local = stays & (k == row)

        @pl.when(local)
        def _():
            pltpu.make_async_copy(here, out_ref.at[at.slot], recv.at[OUT, at.slot]).start()

        @pl.when(jnp.logical_not(local))
        def _():
            remote(here, out_ref.at[at.slot], OUT, k, at.slot, at.source(k)).start()

        return 0

    lax.fori_loop(0, 8, multiply, 0)

    def finish(k, _):
        one = rows(k)

        def sent(kind):
            pltpu.make_async_copy(one, one, send.at[kind, k]).wait()

        @pl.when(jnp.logical_not(stays & (k == at.slot)))
        def _():
            sent(OWN)
            sent(DIN)

        sent(SIB)
        sent(PAIR)
        sent(PAIRF)
        pl.when(has_across)(lambda: sent(YA))
        pl.when(has_ahead)(lambda: sent(YB))
        pl.when(has_behind)(lambda: sent(YBF))
        pl.when(relay_a)(lambda: sent(RAF))

        @pl.when(relay_b & ((k == arrival((at.z - heading + 4) % 4, 0)) | (k == arrival((at.z - heading + 4) % 4, 1))))
        def _():
            sent(RBF)


        @pl.when(jnp.logical_not(stays & (k == row)))
        def _():
            sent(OUT)

        arrived(out_ref.at[k], OUT, k)
        return 0

    lax.fori_loop(0, 8, finish, 0)


def match_index(density_cols, hamilton_cols):
    start = Place().start
    left = lax.dynamic_slice_in_dim(density_cols, start, ROWS, 0)
    right = jnp.take(hamilton_cols, left, axis=0)
    hit = right[:, :, None, :] == left[:, None, :, None]
    n = jnp.arange(LIST, dtype=jnp.int32)
    which = jnp.sum(jnp.where(hit, n, 0), axis=-1)
    block = (left - start + W)[:, :, None] * LIST + which
    return jnp.where(jnp.any(hit, axis=-1), block, WINDOW * LIST).reshape(-1).astype(jnp.int32)


def per_device(density_blocks, hamilton_blocks, density_cols, hamilton_cols):
    index = match_index(density_cols, hamilton_cols)
    block = density_blocks.shape[2:]
    kind = density_blocks.dtype
    return pl.pallas_call(
        kernel,
        out_shape=jax.ShapeDtypeStruct(density_blocks.shape, kind),
        in_specs=[
            pl.BlockSpec(memory_space=pltpu.SMEM),
            pl.BlockSpec(memory_space=pl.ANY),
            pl.BlockSpec(memory_space=pl.ANY),
        ],
        out_specs=pl.BlockSpec(memory_space=pl.ANY),
        scratch_shapes=[
            pltpu.VMEM((WINDOW * LIST + 1, *block), kind),
            pltpu.VMEM((ROWS * LIST, *block), kind),
            pltpu.VMEM((ROWS * LIST, *block), kind),
            pltpu.VMEM(((ROWS + DETOUR) * LIST, *block), kind),
            pltpu.SemaphoreType.DMA((13, 8)),
            pltpu.SemaphoreType.DMA((13, 8)),
        ],
        compiler_params=pltpu.CompilerParams(
            collective_id=0, has_side_effects=True, vmem_limit_bytes=52 << 20
        ),
        name="block_product",
    )(index, density_blocks, hamilton_blocks)


def solution(mesh):
    return jax.shard_map(
        per_device,
        mesh=mesh,
        in_specs=(
            P(("row", "col"), None, None, None),
            P(("row", "col"), None, None, None),
            P(),
            P(),
        ),
        out_specs=P(("row", "col"), None, None, None),
        check_vma=False,
    )
```

```python
import functools

import jax
import jax.numpy as jnp
from jax import lax
from jax.experimental import pallas as pl
from jax.experimental.pallas import tpu as pltpu
from jax.sharding import PartitionSpec as P

W = 24
LIST = 16
ROWS = 8
WINDOW = 2 * W + ROWS
MESH = pl.DeviceIdType.MESH
OWN, SIB, PAIR, PAIRF, YA, YB, YBF, DIN, OUT, RA, RAF, RB, RBF, YP, YPF = range(15)
DETOUR = 2
A_DELAY = 8
D_START = 4
STEPS = 19


def ring(side, i):
    return side * 3 + i * (1 - 2 * side)


def ring_of(group):
    slot = group // 4
    return ring(slot // 4, slot % 4)


class Place:
    def __init__(self):
        self.row = lax.axis_index("row")
        self.col = lax.axis_index("col")
        self.z, self.core = self.row // 2, self.row % 2
        self.y, self.x = self.col // 4, self.col % 4
        self.half = self.x // 2
        self.side = (self.x + self.half) % 2
        self.slot = self.side * 4 + ring(self.side, self.z)
        self.group = self.slot * 4 + self.y
        self.quarter = self.half * 2 + self.core
        self.start = self.group * 32 + self.quarter * 8

    def home(self, slot):
        side = slot // 4
        x = side + self.half * (3 - 2 * side)
        return (ring(side, slot % 4) * 2 + self.x % 2, self.y * 4 + x)

    def source(self, k):
        return (k, self.y * 4 + self.quarter)

    def member(self, group, core):
        slot = group // 4
        side = slot // 4
        x = side + self.half * (3 - 2 * side)
        return (ring(side, slot % 4) * 2 + core, (group % 4) * 4 + x)


def turn(i):
    i = i // 2
    return i + (i // 2) * (1 - 2 * (i % 2))


def arrival(z, j):
    return ((z - turn(j) + 4) % 4) * 2 + j % 2


def kernel(index_ref, d_ref, h_ref, out_ref, window, dbuf, obuf, rbuf, send, recv):
    at = Place()
    row, core = at.row, at.core
    sibling = (at.row + 1 - 2 * core, at.col)
    pair = (at.row, at.y * 4 + 3 - at.x)
    heading = 1 - 2 * at.half
    facing = 2 * core - 1
    across = at.group + facing
    ahead = at.group + heading
    behind = at.group - heading
    has_across = (across >= 0) & (across < 32)
    has_ahead = (ahead >= 0) & (ahead < 32)
    has_behind = (behind >= 0) & (behind < 32)
    across_dev = at.member(across, 1 - core)
    ahead_dev = at.member(ahead, core)
    behind_dev = at.member(behind, core)
    stays = at.x % 2 == core
    def near(slot):
        return (slot >= 0) & (slot < 8)

    def flips(slot):
        return at.slot + slot == 7

    def pick(cond, a, b):
        return jnp.where(cond, a, b)

    seam_a = has_across & (at.y == 3 * core)
    flip_a = flips(at.slot + facing)
    a_next = at.member(at.group + pick(flip_a, -3 * facing, 4 * facing), 1 - core)
    a_from = at.member(at.group + pick(flip_a, 4 * facing, -3 * facing), core)
    turn_a = (at.y == 3 * core) & flips(at.slot - facing)
    relay_a = turn_a | (
        (at.y == 3 - 3 * core) & near(at.slot + facing) & jnp.logical_not(flip_a)
    )
    a_group = at.group + pick(turn_a, -3 * facing, 4 * facing)
    a_last = at.member(a_group, 1 - core)
    a_to = at.member(at.group + pick(turn_a, -4 * facing, 3 * facing), core)
    outer = core == at.half
    inner = core != at.half
    seam_b = has_ahead & outer & (at.y == 3 - 3 * at.half)
    seam_in = has_behind & outer & (at.y == 3 * at.half)
    flip_ahead = flips(at.slot + heading)
    flip_behind = flips(at.slot - heading)
    b_next = at.member(at.group + pick(flip_ahead, -3 * heading, 4 * heading), core)
    from_b = at.member(at.group + pick(flip_behind, -4 * heading, 3 * heading), core)
    turn_b = outer & (at.y == 3 * at.half) & flip_ahead
    relay_b = turn_b | (
        outer & (at.y == 3 - 3 * at.half) & near(at.slot - heading) & jnp.logical_not(flip_behind)
    )
    b_group = at.group + pick(turn_b, 3 * heading, -4 * heading)
    b_last = at.member(b_group, core)
    b_to = at.member(at.group + pick(turn_b, 4 * heading, -3 * heading), core)

    barrier = pltpu.get_barrier_semaphore()

    def greet(dev):
        pl.semaphore_signal(barrier, inc=1, device_id=dev, device_id_type=MESH)

    def greet_slot(i, _):
        @pl.when(jnp.logical_not(stays & (i == at.slot)))
        def _():
            greet(at.home(i))

        @pl.when(jnp.logical_not(stays & (i == row)))
        def _():
            greet(at.source(i))

        return 0

    lax.fori_loop(0, 8, greet_slot, 0)
    greet(sibling)
    greet(pair)
    pl.when(has_across & jnp.logical_not(seam_a))(lambda: greet(across_dev))
    pl.when(seam_a)(lambda: (greet(a_next), greet(a_from)) and None)
    pl.when(relay_a)(lambda: (greet(a_last), greet(a_to)) and None)
    pl.when(seam_b)(lambda: greet(b_next))
    pl.when(seam_in)(lambda: greet(from_b))
    pl.when(relay_b)(lambda: (greet(b_last), greet(b_to)) and None)
    pl.when(has_ahead)(lambda: greet(ahead_dev))
    pl.when(has_behind)(lambda: greet(behind_dev))
    count = (
        18
        - 2 * stays.astype(jnp.int32)
        + has_across.astype(jnp.int32)
        + seam_a.astype(jnp.int32)
        + 2 * relay_a.astype(jnp.int32)
        + seam_b.astype(jnp.int32)
        + seam_in.astype(jnp.int32)
        + 2 * relay_b.astype(jnp.int32)
        + has_ahead.astype(jnp.int32)
        + has_behind.astype(jnp.int32)
    )
    pl.semaphore_wait(barrier, count)

    def rows(w):
        return window.at[pl.ds(w * LIST, LIST)]

    def remote(src, dst, kind, s, r, dev, sent=None):
        return pltpu.make_async_remote_copy(
            src_ref=src,
            dst_ref=dst,
            send_sem=send.at[kind if sent is None else sent, s],
            recv_sem=recv.at[kind, r],
            device_id=dev,
            device_id_type=MESH,
        )

    own = W
    to_sib = own + 8 * facing
    at_pair = own + 16 * heading
    to_pair = own - 16 * heading
    pair_to_sib = own + 16 * heading + 8 * facing
    to_across = own - 24 * facing
    at_ahead = own - 16 * heading
    behind_to_sib = own - 16 * heading + 8 * facing
    across_to_pair = own + 24 * facing - 16 * heading
    from_pair = own - 16 * heading - 8 * facing

    def send_home(src_ref, dst, kind, i):
        side = at.side * (1 - 2 * (i % 2)) + i % 2
        slot = side * 4 + ring(side, (at.z + turn(i)) % 4)
        local = stays & (slot == at.slot)

        @pl.when(local)
        def _():
            pltpu.make_async_copy(src_ref.at[slot], dst, recv.at[kind, row]).start()

        @pl.when(jnp.logical_not(local))
        def _():
            remote(src_ref.at[slot], dst, kind, slot, row, at.home(slot)).start()

    def send_h(i, _):
        send_home(h_ref, rows(own + row), OWN, i)
        return 0

    lax.fori_loop(0, 8, send_h, 0)

    def relayed(i):
        return rbuf.at[pl.ds(i * LIST, LIST)]

    def arrived(ref, kind, k):
        pltpu.make_async_copy(ref, ref, recv.at[kind, k]).wait()

    def step(u, _):
        @pl.when(u < 8)
        def _():
            k = arrival(at.z, u)
            here = rows(own + k)
            arrived(here, OWN, k)
            remote(here, rows(to_pair + k), PAIR, k, k, pair).start()

            @pl.when(has_across & jnp.logical_not(seam_a))
            def _():
                remote(here, rows(to_across + k), YA, k, k, across_dev).start()

            remote(here, rows(to_sib + k), SIB, k, k, sibling).start()

        @pl.when((u >= 3) & (u < 18) & (u % 2 == 1))
        def _():
            j = (u - 3) // 2
            k = arrival(at.z, j)
            here = rows(at_pair + k)
            arrived(here, PAIR, k)
            around = seam_b & (j < DETOUR)

            @pl.when(has_ahead & (outer | (k % 2 == 0)) & jnp.logical_not(around))
            def _():
                remote(here, rows(at_ahead + k), YB, k, k, ahead_dev).start()

            @pl.when(around)
            def _():
                remote(here, relayed(8 + j), RB, k, k, b_next, YB).start()

            remote(here, rows(pair_to_sib + k), PAIRF, k, k, sibling).start()

        @pl.when((u >= A_DELAY) & (u < A_DELAY + 8) & seam_a)
        def _():
            k = arrival(at.z, u - A_DELAY)
            remote(rows(own + k), relayed(k), RA, k, k, a_next, YA).start()

        @pl.when((u >= A_DELAY + 3) & (u < A_DELAY + 11) & relay_a)
        def _():
            k = arrival(ring_of(a_group), u - A_DELAY - 3)
            here = relayed(k)
            arrived(here, RA, k)
            remote(here, rows(own + 24 * facing + k), YA, k, k, a_to, RAF).start()

        @pl.when((u == 7) & relay_b | (u == 9) & relay_b)
        def _():
            j = (u - 7) // 2
            k = arrival(ring_of(b_group), j)
            here = relayed(8 + j)
            arrived(here, RB, k)
            remote(here, rows(at_ahead + k), YB, k, k, b_to, RBF).start()

        @pl.when((u >= 10) & (u < 18) & (u % 2 == 0) & inner & has_across & jnp.logical_not(seam_a))
        def _():
            across_on(u - 9)

        @pl.when((u >= D_START) & (u < D_START + 8))
        def _():
            send_home(d_ref, dbuf.at[pl.ds(row * LIST, LIST)], DIN, u - D_START)

        return 0

    def across_on(i):
        k = arrival(ring_of(across), i)
        here = rows(own + 24 * facing + k)
        arrived(here, YA, k)
        remote(here, rows(across_to_pair + k), YBF, k, k, pair, YP).start()

    lax.fori_loop(0, STEPS, step, 0)

    @pl.when(inner & seam_a)
    def _():
        def body(i, _):
            across_on(2 * i + 1)
            return 0

        lax.fori_loop(0, 4, body, 0)

    def hand_on(j, _):
        k = arrival(ring_of(behind), j)

        @pl.when(outer | (k % 2 == 0))
        def _():
            here = rows(at_ahead + k)
            arrived(here, YB, k)
            remote(here, rows(behind_to_sib + k), YBF, k, k, sibling).start()

        @pl.when(outer & (k % 2 == 1))
        def _():
            here = rows(from_pair + k)
            arrived(here, YBF, k)
            remote(here, rows(at_ahead + k), YB, k, k, sibling, YPF).start()

        return 0

    @pl.when(has_behind)
    def _():
        lax.fori_loop(0, 8, hand_on, 0)

    zero = WINDOW * LIST
    window[zero] = jnp.zeros(window.shape[1:], window.dtype)

    def collect(k, _):
        one = rows(k)
        arrived(one, SIB, k)
        arrived(one, PAIRF, k)

        @pl.when(has_across & (outer | (k % 2 == 0)))
        def _():
            arrived(one, YA, k)

        @pl.when(has_behind & (inner | (k % 2 == 0)))
        def _():
            arrived(one, YBF, k)

        @pl.when(has_behind & inner & (k % 2 == 1))
        def _():
            arrived(one, YB, k)

        arrived(one, DIN, k)
        return 0

    lax.fori_loop(0, 8, collect, 0)

    def multiply(j, _):
        k = arrival(at.z, 7 - j)

        def columns(p, _):
            total = jnp.zeros((128, 256), jnp.float32)
            for m in range(0, LIST, 2):
                left = jnp.concatenate([dbuf[k * LIST + m], dbuf[k * LIST + m + 1]], axis=1)
                base = (k * LIST + m) * LIST + 2 * p
                upper = jnp.concatenate([window[index_ref[base]], window[index_ref[base + 1]]], axis=1)
                lower = jnp.concatenate(
                    [window[index_ref[base + LIST]], window[index_ref[base + LIST + 1]]], axis=1
                )
                right = jnp.concatenate([upper, lower], axis=0)
                total = total + jnp.dot(left, right, preferred_element_type=jnp.float32)
            obuf[k * LIST + 2 * p] = total[:, :128].astype(obuf.dtype)
            obuf[k * LIST + 2 * p + 1] = total[:, 128:].astype(obuf.dtype)
            return 0

        lax.fori_loop(0, LIST // 2, columns, 0)
        here = obuf.at[pl.ds(k * LIST, LIST)]
        local = stays & (k == row)

        @pl.when(local)
        def _():
            pltpu.make_async_copy(here, out_ref.at[at.slot], recv.at[OUT, at.slot]).start()

        @pl.when(jnp.logical_not(local))
        def _():
            remote(here, out_ref.at[at.slot], OUT, k, at.slot, at.source(k)).start()

        return 0

    lax.fori_loop(0, 8, multiply, 0)

    def finish(k, _):
        one = rows(k)

        def sent(kind):
            pltpu.make_async_copy(one, one, send.at[kind, k]).wait()

        @pl.when(jnp.logical_not(stays & (k == at.slot)))
        def _():
            sent(OWN)
            sent(DIN)

        sent(SIB)
        sent(PAIR)
        sent(PAIRF)
        pl.when(has_across)(lambda: sent(YA))
        pl.when(has_ahead & (outer | (k % 2 == 0)))(lambda: sent(YB))
        pl.when(has_behind & (outer | (k % 2 == 0)))(lambda: sent(YBF))
        pl.when(has_across & inner & (k % 2 == 1))(lambda: sent(YP))
        pl.when(has_behind & outer & (k % 2 == 1))(lambda: sent(YPF))
        pl.when(relay_a)(lambda: sent(RAF))

        @pl.when(relay_b & ((k == arrival(ring_of(b_group), 0)) | (k == arrival(ring_of(b_group), 1))))
        def _():
            sent(RBF)


        @pl.when(jnp.logical_not(stays & (k == row)))
        def _():
            sent(OUT)

        arrived(out_ref.at[k], OUT, k)
        return 0

    lax.fori_loop(0, 8, finish, 0)


def match_index(density_cols, hamilton_cols):
    start = Place().start
    left = lax.dynamic_slice_in_dim(density_cols, start, ROWS, 0)
    right = jnp.take(hamilton_cols, left, axis=0)
    hit = right[:, :, None, :] == left[:, None, :, None]
    n = jnp.arange(LIST, dtype=jnp.int32)
    which = jnp.sum(jnp.where(hit, n, 0), axis=-1)
    block = (left - start + W)[:, :, None] * LIST + which
    return jnp.where(jnp.any(hit, axis=-1), block, WINDOW * LIST).reshape(-1).astype(jnp.int32)


def per_device(density_blocks, hamilton_blocks, density_cols, hamilton_cols):
    index = match_index(density_cols, hamilton_cols)
    block = density_blocks.shape[2:]
    kind = density_blocks.dtype
    return pl.pallas_call(
        kernel,
        out_shape=jax.ShapeDtypeStruct(density_blocks.shape, kind),
        in_specs=[
            pl.BlockSpec(memory_space=pltpu.SMEM),
            pl.BlockSpec(memory_space=pl.ANY),
            pl.BlockSpec(memory_space=pl.ANY),
        ],
        out_specs=pl.BlockSpec(memory_space=pl.ANY),
        scratch_shapes=[
            pltpu.VMEM((WINDOW * LIST + 1, *block), kind),
            pltpu.VMEM((ROWS * LIST, *block), kind),
            pltpu.VMEM((ROWS * LIST, *block), kind),
            pltpu.VMEM(((ROWS + DETOUR) * LIST, *block), kind),
            pltpu.SemaphoreType.DMA((15, 8)),
            pltpu.SemaphoreType.DMA((15, 8)),
        ],
        compiler_params=pltpu.CompilerParams(
            collective_id=0, has_side_effects=True, vmem_limit_bytes=52 << 20
        ),
        name="block_product",
    )(index, density_blocks, hamilton_blocks)


def solution(mesh):
    return jax.shard_map(
        per_device,
        mesh=mesh,
        in_specs=(
            P(("row", "col"), None, None, None),
            P(("row", "col"), None, None, None),
            P(),
            P(),
        ),
        out_specs=P(("row", "col"), None, None, None),
        check_vma=False,
    )
```

```python
import jax
import jax.numpy as jnp
from jax import lax
from jax.experimental import pallas as pl
from jax.experimental.pallas import tpu as pltpu
from jax.sharding import PartitionSpec as P

W = 24
LIST = 16
ROWS = 8
WINDOW = 2 * W + ROWS
MESH = pl.DeviceIdType.MESH
OWN, SIB, PAIR, PAIRF, YA, YB, YBF, DIN, OUT, RB, RBF, YP, YPF = range(13)
PARTS = 2
PIECES = ROWS * PARTS
SIZE = LIST // PARTS
DETOUR = 8 * PARTS
D_START = 9 * PARTS
PAIR_START = 3
RELAY_LAG = 12
RELAY_WAIT = 10
YP_LATE = 4
HOLD = 8
YA_HOLD = 16
YP_START = PIECES + 1
STEPS = max(PAIR_START + 2 * PIECES, YP_START + YP_LATE + PIECES, PAIR_START + RELAY_WAIT + 2 * PIECES)


def ring(side, i):
    return side * 3 + i * (1 - 2 * side)


def ring_of(group):
    slot = group // 4
    return ring(slot // 4, slot % 4)


class Place:
    def __init__(self):
        self.row = lax.axis_index("row")
        self.col = lax.axis_index("col")
        self.z, self.core = self.row // 2, self.row % 2
        self.y, self.x = self.col // 4, self.col % 4
        self.half = self.x // 2
        self.side = (self.x + self.half) % 2
        self.slot = self.side * 4 + ring(self.side, self.z)
        self.group = self.slot * 4 + self.y
        self.quarter = self.half * 2 + self.core
        self.start = self.group * 32 + self.quarter * 8

    def home(self, slot):
        side = slot // 4
        x = side + self.half * (3 - 2 * side)
        return (ring(side, slot % 4) * 2 + self.x % 2, self.y * 4 + x)

    def source(self, k):
        return (k, self.y * 4 + self.quarter)

    def member(self, group, core):
        slot = group // 4
        side = slot // 4
        x = side + self.half * (3 - 2 * side)
        return (ring(side, slot % 4) * 2 + core, (group % 4) * 4 + x)


def turn(i):
    i = i // 2
    return i + (i // 2) * (1 - 2 * (i % 2))


def arrival(z, j):
    i = j // PARTS
    return (((z - turn(i) + 4) % 4) * 2 + i % 2) * PARTS + j % PARTS


def kernel(index_ref, d_ref, h_ref, out_ref, window, dbuf, obuf, rbuf, send, recv):
    at = Place()
    row, core = at.row, at.core
    sibling = (at.row + 1 - 2 * core, at.col)
    pair = (at.row, at.y * 4 + 3 - at.x)
    heading = 1 - 2 * at.half
    facing = 2 * core - 1
    across = at.group + facing
    ahead = at.group + heading
    behind = at.group - heading
    has_across = (across >= 0) & (across < 32)
    has_ahead = (ahead >= 0) & (ahead < 32)
    has_behind = (behind >= 0) & (behind < 32)
    across_dev = at.member(across, 1 - core)
    ahead_dev = at.member(ahead, core)
    behind_dev = at.member(behind, core)
    stays = at.x % 2 == core
    def near(slot):
        return (slot >= 0) & (slot < 8)

    def flips(slot):
        return at.slot + slot == 7

    def pick(cond, a, b):
        return jnp.where(cond, a, b)

    seam_a = has_across & (at.y == 3 * core)
    held_a = seam_a & jnp.logical_not(flips(at.slot + facing))
    seam_ahead = has_ahead & (at.y == 3 - 3 * at.half)
    seam_behind = has_behind & (at.y == 3 * at.half)
    outer = core == at.half
    inner = core != at.half
    seam_b = seam_ahead & outer
    seam_in = seam_behind & outer
    flip_ahead = flips(at.slot + heading)
    flip_behind = flips(at.slot - heading)
    b_next = at.member(at.group + pick(flip_ahead, -3 * heading, 4 * heading), core)
    from_b = at.member(at.group + pick(flip_behind, -4 * heading, 3 * heading), core)
    turn_b = outer & (at.y == 3 * at.half) & flip_ahead
    relay_b = turn_b | (
        outer & (at.y == 3 - 3 * at.half) & near(at.slot - heading) & jnp.logical_not(flip_behind)
    )
    b_group = at.group + pick(turn_b, 3 * heading, -4 * heading)
    b_last = at.member(b_group, core)
    b_to = at.member(at.group + pick(turn_b, 4 * heading, -3 * heading), core)

    relays = DETOUR
    turns = DETOUR

    barrier = pltpu.get_barrier_semaphore()

    def greet(dev):
        pl.semaphore_signal(barrier, inc=1, device_id=dev, device_id_type=MESH)

    def greet_slot(i, _):
        @pl.when(jnp.logical_not(stays & (i == at.slot)))
        def _():
            greet(at.home(i))

        @pl.when(jnp.logical_not(stays & (i == row)))
        def _():
            greet(at.source(i))

        return 0

    lax.fori_loop(0, 8, greet_slot, 0)
    greet(sibling)
    greet(pair)
    pl.when(has_across)(lambda: greet(across_dev))
    pl.when(seam_b)(lambda: greet(b_next))
    pl.when(seam_in)(lambda: greet(from_b))
    pl.when(relay_b)(lambda: (greet(b_last), greet(b_to)) and None)
    pl.when(has_ahead)(lambda: greet(ahead_dev))
    pl.when(has_behind)(lambda: greet(behind_dev))
    count = (
        18
        - 2 * stays.astype(jnp.int32)
        + has_across.astype(jnp.int32)
        + seam_b.astype(jnp.int32)
        + seam_in.astype(jnp.int32)
        + 2 * relay_b.astype(jnp.int32)
        + has_ahead.astype(jnp.int32)
        + has_behind.astype(jnp.int32)
    )
    pl.semaphore_wait(barrier, count)

    def rows(w):
        return window.at[pl.ds(w * SIZE, SIZE)]

    def remote(src, dst, kind, s, r, dev, sent=None):
        return pltpu.make_async_remote_copy(
            src_ref=src,
            dst_ref=dst,
            send_sem=send.at[kind if sent is None else sent, s],
            recv_sem=recv.at[kind, r],
            device_id=dev,
            device_id_type=MESH,
        )

    one = PARTS
    own = W * one
    to_sib = own + 8 * one * facing
    at_pair = own + 16 * one * heading
    to_pair = own - 16 * one * heading
    pair_to_sib = own + 16 * one * heading + 8 * one * facing
    to_across = own - 24 * one * facing
    at_ahead = own - 16 * one * heading
    behind_to_sib = own - 16 * one * heading + 8 * one * facing
    across_to_pair = own + 24 * one * facing - 16 * one * heading
    from_pair = own - 16 * one * heading - 8 * one * facing

    def send_home(src_ref, buf, base, kind, i):
        part = i % PARTS
        i = i // PARTS
        side = at.side * (1 - 2 * (i % 2)) + i % 2
        slot = side * 4 + ring(side, (at.z + turn(i)) % 4)
        local = stays & (slot == at.slot)
        piece = row * PARTS + part
        src = src_ref.at[slot, pl.ds(part * SIZE, SIZE)]
        dst = buf.at[pl.ds((base + piece) * SIZE, SIZE)]

        @pl.when(local)
        def _():
            pltpu.make_async_copy(src, dst, recv.at[kind, piece]).start()

        @pl.when(jnp.logical_not(local))
        def _():
            remote(src, dst, kind, slot * PARTS + part, piece, at.home(slot)).start()

    def send_h(i, _):
        send_home(h_ref, window, own, OWN, i)
        return 0

    lax.fori_loop(0, PIECES, send_h, 0)

    def send_d(i, _):
        send_home(d_ref, dbuf, 0, DIN, PIECES - 1 - i)
        return 0

    def shared(k, seam):
        return (k % 2 == 1) | (seam & (k % 4 == 0))


    def relayed(i):
        return rbuf.at[pl.ds(i * SIZE, SIZE)]

    def arrived(ref, kind, k):
        pltpu.make_async_copy(ref, ref, recv.at[kind, k]).wait()

    def send_across(j):
        k = arrival(at.z, j)
        remote(rows(own + k), rows(to_across + k), YA, k, k, across_dev).start()

    def send_held_across(j, _):
        send_across(j)
        return 0

    def across_on(k):
        here = rows(own + 24 * one * facing + k)
        arrived(here, YA, k)
        remote(here, rows(across_to_pair + k), YBF, k, k, pair, YP).start()

    def send_ahead(j):
        k = arrival(at.z, j)
        here = rows(at_pair + k)
        around = seam_b & (j < turns)

        @pl.when(has_ahead & (outer | jnp.logical_not(shared(k, seam_ahead))) & jnp.logical_not(around))
        def _():
            remote(here, rows(at_ahead + k), YB, k, k, ahead_dev).start()

        @pl.when(around)
        def _():
            remote(here, relayed(j), RB, k, k, b_next, YB).start()

    def send_held(j, _):
        send_ahead(j)
        return 0

    def step(u, _):
        @pl.when(u < PIECES)
        def _():
            k = arrival(at.z, u)
            here = rows(own + k)
            arrived(here, OWN, k)
            remote(here, rows(to_pair + k), PAIR, k, k, pair).start()

            pl.when(has_across & (jnp.logical_not(held_a) | (u >= YA_HOLD)))(lambda: send_across(u))

            remote(here, rows(to_sib + k), SIB, k, k, sibling).start()

        @pl.when((u >= PAIR_START) & (u < PAIR_START + 2 * PIECES) & ((u - PAIR_START) % 2 == 0))
        def _():
            j = (u - PAIR_START) // 2
            k = arrival(at.z, j)
            here = rows(at_pair + k)
            arrived(here, PAIR, k)

            @pl.when(jnp.logical_not(seam_ahead) | (u >= HOLD))
            def _():
                send_ahead(j)

            remote(here, rows(pair_to_sib + k), PAIRF, k, k, sibling).start()

        @pl.when((u == YA_HOLD - 1) & held_a)
        def _():
            lax.fori_loop(0, YA_HOLD, send_held_across, 0)

        @pl.when((u == HOLD) & seam_ahead)
        def _():
            lax.fori_loop(0, (HOLD - PAIR_START + 1) // 2, send_held, 0)

        first = HOLD + RELAY_LAG
        slow = PAIR_START + RELAY_WAIT
        bend = first - slow
        early = (u >= first) & (u < first + bend)
        later = (u >= first + bend) & ((u - slow) % 2 == 0) & (u < slow + 2 * DETOUR)

        @pl.when((early | later) & relay_b)
        def _():
            j = pick(early, u - first, (u - slow) // 2)
            k = arrival(ring_of(b_group), j)
            here = relayed(j)
            arrived(here, RB, k)
            remote(here, rows(at_ahead + k), YB, k, k, b_to, RBF).start()

        turn_p = u - YP_START - pick(seam_a, YP_LATE, 0)

        @pl.when((turn_p >= 0) & (turn_p < PIECES) & inner & has_across)
        def _():
            k = arrival(ring_of(across), turn_p)
            pl.when(shared(k, seam_a))(lambda: across_on(k))

        @pl.when(u == D_START)
        def _():
            lax.fori_loop(0, PIECES, send_d, 0)

        return 0

    lax.fori_loop(0, STEPS, step, 0)

    def hand_on(j, _):
        k = arrival(ring_of(behind), j)

        @pl.when(outer | jnp.logical_not(shared(k, seam_behind)))
        def _():
            here = rows(at_ahead + k)
            arrived(here, YB, k)
            remote(here, rows(behind_to_sib + k), YBF, k, k, sibling).start()

        @pl.when(outer & shared(k, seam_behind))
        def _():
            here = rows(from_pair + k)
            arrived(here, YBF, k)
            remote(here, rows(at_ahead + k), YB, k, k, sibling, YPF).start()

        return 0

    @pl.when(has_behind)
    def _():
        lax.fori_loop(0, PIECES, hand_on, 0)

    zero = WINDOW * LIST
    window[zero] = jnp.zeros(window.shape[1:], window.dtype)

    def collect(k, _):
        one = rows(k)
        arrived(one, SIB, k)
        arrived(one, PAIRF, k)

        @pl.when(has_across & (outer | jnp.logical_not(shared(k, seam_a))))
        def _():
            arrived(one, YA, k)

        @pl.when(has_behind & (inner | jnp.logical_not(shared(k, seam_behind))))
        def _():
            arrived(one, YBF, k)

        @pl.when(has_behind & inner & shared(k, seam_behind))
        def _():
            arrived(one, YB, k)

        return 0

    lax.fori_loop(0, PIECES, collect, 0)

    def multiply(j, _):
        piece = arrival(at.z, PIECES - 1 - j)
        k = piece // PARTS
        part = piece % PARTS

        @pl.when(j % PARTS == 0)
        def _():
            for i in range(PARTS):
                arrived(rows(k * PARTS + i), DIN, k * PARTS + i)

        def columns(i, _):
            p = part * (SIZE // 2) + i
            total = jnp.zeros((128, 256), jnp.float32)
            for m in range(0, LIST, 2):
                left = jnp.concatenate([dbuf[k * LIST + m], dbuf[k * LIST + m + 1]], axis=1)
                base = (k * LIST + m) * LIST + 2 * p
                upper = jnp.concatenate([window[index_ref[base]], window[index_ref[base + 1]]], axis=1)
                lower = jnp.concatenate(
                    [window[index_ref[base + LIST]], window[index_ref[base + LIST + 1]]], axis=1
                )
                right = jnp.concatenate([upper, lower], axis=0)
                total = total + jnp.dot(left, right, preferred_element_type=jnp.float32)
            obuf[k * LIST + 2 * p] = total[:, :128].astype(obuf.dtype)
            obuf[k * LIST + 2 * p + 1] = total[:, 128:].astype(obuf.dtype)
            return 0

        lax.fori_loop(0, SIZE // 2, columns, 0)
        here = obuf.at[pl.ds(piece * SIZE, SIZE)]
        there = out_ref.at[at.slot, pl.ds(part * SIZE, SIZE)]
        place = at.slot * PARTS + part
        local = stays & (k == row)

        @pl.when(local)
        def _():
            pltpu.make_async_copy(here, there, recv.at[OUT, place]).start()

        @pl.when(jnp.logical_not(local))
        def _():
            remote(here, there, OUT, piece, place, at.source(k)).start()

        return 0

    lax.fori_loop(0, PIECES, multiply, 0)

    def finish(k, _):
        one = rows(k)

        def sent(kind):
            pltpu.make_async_copy(one, one, send.at[kind, k]).wait()

        @pl.when(jnp.logical_not(stays & (k // PARTS == at.slot)))
        def _():
            sent(OWN)
            sent(DIN)

        sent(SIB)
        sent(PAIR)
        sent(PAIRF)
        pl.when(has_across)(lambda: sent(YA))
        pl.when(has_ahead & (outer | jnp.logical_not(shared(k, seam_ahead))))(lambda: sent(YB))
        pl.when(has_behind & (outer | jnp.logical_not(shared(k, seam_behind))))(lambda: sent(YBF))
        pl.when(has_across & inner & shared(k, seam_a))(lambda: sent(YP))
        pl.when(has_behind & outer & shared(k, seam_behind))(lambda: sent(YPF))
        by_relay = relay_b & (k < 0)
        for j in range(PIECES):
            by_relay = by_relay | (relay_b & (j < relays) & (k == arrival(ring_of(b_group), j)))
        pl.when(by_relay)(lambda: sent(RBF))

        @pl.when(jnp.logical_not(stays & (k // PARTS == row)))
        def _():
            sent(OUT)

        arrived(out_ref.at[k // PARTS, pl.ds((k % PARTS) * SIZE, SIZE)], OUT, k)
        return 0

    lax.fori_loop(0, PIECES, finish, 0)


def match_index(density_cols, hamilton_cols):
    start = Place().start
    left = lax.dynamic_slice_in_dim(density_cols, start, ROWS, 0)
    right = jnp.take(hamilton_cols, left, axis=0)
    hit = right[:, :, None, :] == left[:, None, :, None]
    n = jnp.arange(LIST, dtype=jnp.int32)
    which = jnp.sum(jnp.where(hit, n, 0), axis=-1)
    block = (left - start + W)[:, :, None] * LIST + which
    return jnp.where(jnp.any(hit, axis=-1), block, WINDOW * LIST).reshape(-1).astype(jnp.int32)


def per_device(density_blocks, hamilton_blocks, density_cols, hamilton_cols):
    index = match_index(density_cols, hamilton_cols)
    block = density_blocks.shape[2:]
    kind = density_blocks.dtype
    return pl.pallas_call(
        kernel,
        out_shape=jax.ShapeDtypeStruct(density_blocks.shape, kind),
        in_specs=[
            pl.BlockSpec(memory_space=pltpu.SMEM),
            pl.BlockSpec(memory_space=pl.ANY),
            pl.BlockSpec(memory_space=pl.ANY),
        ],
        out_specs=pl.BlockSpec(memory_space=pl.ANY),
        scratch_shapes=[
            pltpu.VMEM((WINDOW * LIST + 1, *block), kind),
            pltpu.VMEM((ROWS * LIST, *block), kind),
            pltpu.VMEM((ROWS * LIST, *block), kind),
            pltpu.VMEM((PIECES * SIZE, *block), kind),
            pltpu.SemaphoreType.DMA((13, PIECES)),
            pltpu.SemaphoreType.DMA((13, PIECES)),
        ],
        compiler_params=pltpu.CompilerParams(
            collective_id=0, has_side_effects=True, vmem_limit_bytes=52 << 20
        ),
        name="block_product",
    )(index, density_blocks, hamilton_blocks)


def solution(mesh):
    return jax.shard_map(
        per_device,
        mesh=mesh,
        in_specs=(
            P(("row", "col"), None, None, None),
            P(("row", "col"), None, None, None),
            P(),
            P(),
        ),
        out_specs=P(("row", "col"), None, None, None),
        check_vma=False,
    )
```

```python
import jax
import jax.numpy as jnp
from jax import lax
from jax.experimental import pallas as pl
from jax.experimental.pallas import tpu as pltpu
from jax.sharding import PartitionSpec as P

W = 24
LIST = 16
ROWS = 8
WINDOW = 2 * W + ROWS
MESH = pl.DeviceIdType.MESH
OWN, SIB, PAIR, PAIRF, YA, YB, YBF, DIN, OUT, RB, RBF, YP, YPF = range(13)
PARTS = 2
PIECES = ROWS * PARTS
SIZE = LIST // PARTS
DETOUR = 8 * PARTS
D_START = 9 * PARTS
D_BATCH = 4
D_GAP = 4
PAIR_START = 3
RELAY_LAG = 12
RELAY_WAIT = 10
YP_LATE = 4
SEAM_S = 4
HOLD = 8
YA_HOLD = 16
YP_START = PIECES + 1
STEPS = max(PAIR_START + 2 * PIECES, YP_START + YP_LATE + PIECES, PAIR_START + RELAY_WAIT + 2 * PIECES)


def ring(side, i):
    return side * 3 + i * (1 - 2 * side)


def ring_of(group):
    slot = group // 4
    return ring(slot // 4, slot % 4)


class Place:
    def __init__(self):
        self.row = lax.axis_index("row")
        self.col = lax.axis_index("col")
        self.z, self.core = self.row // 2, self.row % 2
        self.y, self.x = self.col // 4, self.col % 4
        self.half = self.x // 2
        self.side = (self.x + self.half) % 2
        self.slot = self.side * 4 + ring(self.side, self.z)
        self.group = self.slot * 4 + self.y
        self.quarter = self.half * 2 + self.core
        self.start = self.group * 32 + self.quarter * 8

    def home(self, slot):
        side = slot // 4
        x = side + self.half * (3 - 2 * side)
        return (ring(side, slot % 4) * 2 + self.x % 2, self.y * 4 + x)

    def source(self, k):
        return (k, self.y * 4 + self.quarter)

    def member(self, group, core):
        slot = group // 4
        side = slot // 4
        x = side + self.half * (3 - 2 * side)
        return (ring(side, slot % 4) * 2 + core, (group % 4) * 4 + x)


def turn(i):
    i = i // 2
    return i + (i // 2) * (1 - 2 * (i % 2))


def arrival(z, j):
    i = j // PARTS
    return (((z - turn(i) + 4) % 4) * 2 + i % 2) * PARTS + j % PARTS


def kernel(index_ref, d_ref, h_ref, out_ref, window, dbuf, obuf, rbuf, send, recv):
    at = Place()
    row, core = at.row, at.core
    sibling = (at.row + 1 - 2 * core, at.col)
    pair = (at.row, at.y * 4 + 3 - at.x)
    heading = 1 - 2 * at.half
    facing = 2 * core - 1
    across = at.group + facing
    ahead = at.group + heading
    behind = at.group - heading
    has_across = (across >= 0) & (across < 32)
    has_ahead = (ahead >= 0) & (ahead < 32)
    has_behind = (behind >= 0) & (behind < 32)
    across_dev = at.member(across, 1 - core)
    ahead_dev = at.member(ahead, core)
    behind_dev = at.member(behind, core)
    stays = at.x % 2 == core
    def near(slot):
        return (slot >= 0) & (slot < 8)

    def flips(slot):
        return at.slot + slot == 7

    def pick(cond, a, b):
        return jnp.where(cond, a, b)

    seam_a = has_across & (at.y == 3 * core)
    held_a = seam_a & jnp.logical_not(flips(at.slot + facing))
    seam_ahead = has_ahead & (at.y == 3 - 3 * at.half)
    seam_behind = has_behind & (at.y == 3 * at.half)
    outer = core == at.half
    inner = core != at.half
    seam_b = seam_ahead & outer
    seam_in = seam_behind & outer
    flip_ahead = flips(at.slot + heading)
    flip_behind = flips(at.slot - heading)
    b_next = at.member(at.group + pick(flip_ahead, -3 * heading, 4 * heading), core)
    from_b = at.member(at.group + pick(flip_behind, -4 * heading, 3 * heading), core)
    turn_b = outer & (at.y == 3 * at.half) & flip_ahead
    relay_b = turn_b | (
        outer & (at.y == 3 - 3 * at.half) & near(at.slot - heading) & jnp.logical_not(flip_behind)
    )
    b_group = at.group + pick(turn_b, 3 * heading, -4 * heading)
    b_last = at.member(b_group, core)
    b_to = at.member(at.group + pick(turn_b, 4 * heading, -3 * heading), core)

    relays = DETOUR
    turns = DETOUR

    barrier = pltpu.get_barrier_semaphore()

    def greet(dev):
        pl.semaphore_signal(barrier, inc=1, device_id=dev, device_id_type=MESH)

    def greet_slot(i, _):
        @pl.when(jnp.logical_not(stays & (i == at.slot)))
        def _():
            greet(at.home(i))

        @pl.when(jnp.logical_not(stays & (i == row)))
        def _():
            greet(at.source(i))

        return 0

    lax.fori_loop(0, 8, greet_slot, 0)
    greet(sibling)
    greet(pair)
    pl.when(has_across)(lambda: greet(across_dev))
    pl.when(seam_b)(lambda: greet(b_next))
    pl.when(seam_in)(lambda: greet(from_b))
    pl.when(relay_b)(lambda: (greet(b_last), greet(b_to)) and None)
    pl.when(has_ahead)(lambda: greet(ahead_dev))
    pl.when(has_behind)(lambda: greet(behind_dev))
    count = (
        18
        - 2 * stays.astype(jnp.int32)
        + has_across.astype(jnp.int32)
        + seam_b.astype(jnp.int32)
        + seam_in.astype(jnp.int32)
        + 2 * relay_b.astype(jnp.int32)
        + has_ahead.astype(jnp.int32)
        + has_behind.astype(jnp.int32)
    )
    pl.semaphore_wait(barrier, count)

    def rows(w):
        return window.at[pl.ds(w * SIZE, SIZE)]

    def remote(src, dst, kind, s, r, dev, sent=None):
        return pltpu.make_async_remote_copy(
            src_ref=src,
            dst_ref=dst,
            send_sem=send.at[kind if sent is None else sent, s],
            recv_sem=recv.at[kind, r],
            device_id=dev,
            device_id_type=MESH,
        )

    one = PARTS
    own = W * one
    to_sib = own + 8 * one * facing
    at_pair = own + 16 * one * heading
    to_pair = own - 16 * one * heading
    pair_to_sib = own + 16 * one * heading + 8 * one * facing
    to_across = own - 24 * one * facing
    at_ahead = own - 16 * one * heading
    behind_to_sib = own - 16 * one * heading + 8 * one * facing
    across_to_pair = own + 24 * one * facing - 16 * one * heading
    from_pair = own - 16 * one * heading - 8 * one * facing

    def send_home(src_ref, buf, base, kind, i):
        part = i % PARTS
        i = i // PARTS
        side = at.side * (1 - 2 * (i % 2)) + i % 2
        slot = side * 4 + ring(side, (at.z + turn(i)) % 4)
        local = stays & (slot == at.slot)
        piece = row * PARTS + part
        src = src_ref.at[slot, pl.ds(part * SIZE, SIZE)]
        dst = buf.at[pl.ds((base + piece) * SIZE, SIZE)]

        @pl.when(local)
        def _():
            pltpu.make_async_copy(src, dst, recv.at[kind, piece]).start()

        @pl.when(jnp.logical_not(local))
        def _():
            remote(src, dst, kind, slot * PARTS + part, piece, at.home(slot)).start()

    def send_h(i, _):
        send_home(h_ref, window, own, OWN, i)
        return 0

    lax.fori_loop(0, PIECES, send_h, 0)

    def send_d(i, _):
        send_home(d_ref, dbuf, 0, DIN, PIECES - 1 - i)
        return 0

    def shared(k, seam):
        return (k % 2 == 1) | (seam & (k % SEAM_S == 0))


    def relayed(i):
        return rbuf.at[pl.ds(i * SIZE, SIZE)]

    def arrived(ref, kind, k):
        pltpu.make_async_copy(ref, ref, recv.at[kind, k]).wait()

    def send_across(j):
        k = arrival(at.z, j)
        remote(rows(own + k), rows(to_across + k), YA, k, k, across_dev).start()

    def send_held_across(j, _):
        send_across(j)
        return 0

    def across_on(k):
        here = rows(own + 24 * one * facing + k)
        arrived(here, YA, k)
        remote(here, rows(across_to_pair + k), YBF, k, k, pair, YP).start()

    def send_ahead(j):
        k = arrival(at.z, j)
        here = rows(at_pair + k)
        around = seam_b & (j < turns)

        @pl.when(has_ahead & (outer | jnp.logical_not(shared(k, seam_ahead))) & jnp.logical_not(around))
        def _():
            remote(here, rows(at_ahead + k), YB, k, k, ahead_dev).start()

        @pl.when(around)
        def _():
            remote(here, relayed(j), RB, k, k, b_next, YB).start()

    def send_held(j, _):
        send_ahead(j)
        return 0

    def step(u, _):
        @pl.when(u < PIECES)
        def _():
            k = arrival(at.z, u)
            here = rows(own + k)
            arrived(here, OWN, k)
            remote(here, rows(to_pair + k), PAIR, k, k, pair).start()

            pl.when(has_across & (jnp.logical_not(held_a) | (u >= YA_HOLD)))(lambda: send_across(u))

            remote(here, rows(to_sib + k), SIB, k, k, sibling).start()

        @pl.when((u >= PAIR_START) & (u < PAIR_START + 2 * PIECES) & ((u - PAIR_START) % 2 == 0))
        def _():
            j = (u - PAIR_START) // 2
            k = arrival(at.z, j)
            here = rows(at_pair + k)
            arrived(here, PAIR, k)

            @pl.when(jnp.logical_not(seam_ahead) | (u >= HOLD))
            def _():
                send_ahead(j)

            remote(here, rows(pair_to_sib + k), PAIRF, k, k, sibling).start()

        @pl.when((u == YA_HOLD - 1) & held_a)
        def _():
            lax.fori_loop(0, YA_HOLD, send_held_across, 0)

        @pl.when((u == HOLD) & seam_ahead)
        def _():
            lax.fori_loop(0, (HOLD - PAIR_START + 1) // 2, send_held, 0)

        first = HOLD + RELAY_LAG
        slow = PAIR_START + RELAY_WAIT
        bend = first - slow
        early = (u >= first) & (u < first + bend)
        later = (u >= first + bend) & ((u - slow) % 2 == 0) & (u < slow + 2 * DETOUR)

        @pl.when((early | later) & relay_b)
        def _():
            j = pick(early, u - first, (u - slow) // 2)
            k = arrival(ring_of(b_group), j)
            here = relayed(j)
            arrived(here, RB, k)
            remote(here, rows(at_ahead + k), YB, k, k, b_to, RBF).start()

        turn_p = u - YP_START - pick(seam_a, YP_LATE, 0)

        @pl.when((turn_p >= 0) & (turn_p < PIECES) & inner & has_across)
        def _():
            k = arrival(ring_of(across), turn_p)
            pl.when(shared(k, seam_a))(lambda: across_on(k))

        batch = (u - D_START) // D_GAP

        @pl.when((u >= D_START) & ((u - D_START) % D_GAP == 0) & (batch < PIECES // D_BATCH))
        def _():
            lax.fori_loop(batch * D_BATCH, (batch + 1) * D_BATCH, send_d, 0)

        return 0

    lax.fori_loop(0, STEPS, step, 0)

    def hand_on(j, _):
        k = arrival(ring_of(behind), j)

        @pl.when(outer | jnp.logical_not(shared(k, seam_behind)))
        def _():
            here = rows(at_ahead + k)
            arrived(here, YB, k)
            remote(here, rows(behind_to_sib + k), YBF, k, k, sibling).start()

        @pl.when(outer & shared(k, seam_behind))
        def _():
            here = rows(from_pair + k)
            arrived(here, YBF, k)
            remote(here, rows(at_ahead + k), YB, k, k, sibling, YPF).start()

        return 0

    @pl.when(has_behind)
    def _():
        lax.fori_loop(0, PIECES, hand_on, 0)

    zero = WINDOW * LIST
    window[zero] = jnp.zeros(window.shape[1:], window.dtype)

    def collect(k, _):
        one = rows(k)
        arrived(one, SIB, k)
        arrived(one, PAIRF, k)

        @pl.when(has_across & (outer | jnp.logical_not(shared(k, seam_a))))
        def _():
            arrived(one, YA, k)

        @pl.when(has_behind & (inner | jnp.logical_not(shared(k, seam_behind))))
        def _():
            arrived(one, YBF, k)

        @pl.when(has_behind & inner & shared(k, seam_behind))
        def _():
            arrived(one, YB, k)

        return 0

    lax.fori_loop(0, PIECES, collect, 0)

    def multiply(j, _):
        piece = arrival(at.z, PIECES - 1 - j)
        k = piece // PARTS
        part = piece % PARTS

        @pl.when(j % PARTS == 0)
        def _():
            for i in range(PARTS):
                arrived(rows(k * PARTS + i), DIN, k * PARTS + i)

        def columns(i, _):
            p = part * (SIZE // 2) + i
            total = jnp.zeros((128, 256), jnp.float32)
            for m in range(0, LIST, 2):
                left = jnp.concatenate([dbuf[k * LIST + m], dbuf[k * LIST + m + 1]], axis=1)
                met = [
                    [window[index_ref[2 * p + q, k * LIST + m + i]] for q in (0, 1)] for i in (0, 1)
                ]
                right = jnp.concatenate([jnp.concatenate(one, axis=1) for one in met], axis=0)
                total = total + jnp.dot(left, right, preferred_element_type=jnp.float32)
            obuf[k * LIST + 2 * p] = total[:, :128].astype(obuf.dtype)
            obuf[k * LIST + 2 * p + 1] = total[:, 128:].astype(obuf.dtype)
            return 0

        lax.fori_loop(0, SIZE // 2, columns, 0)
        here = obuf.at[pl.ds(piece * SIZE, SIZE)]
        there = out_ref.at[at.slot, pl.ds(part * SIZE, SIZE)]
        place = at.slot * PARTS + part
        local = stays & (k == row)

        @pl.when(local)
        def _():
            pltpu.make_async_copy(here, there, recv.at[OUT, place]).start()

        @pl.when(jnp.logical_not(local))
        def _():
            remote(here, there, OUT, piece, place, at.source(k)).start()

        return 0

    lax.fori_loop(0, PIECES, multiply, 0)

    def finish(k, _):
        one = rows(k)

        def sent(kind):
            pltpu.make_async_copy(one, one, send.at[kind, k]).wait()

        @pl.when(jnp.logical_not(stays & (k // PARTS == at.slot)))
        def _():
            sent(OWN)
            sent(DIN)

        sent(SIB)
        sent(PAIR)
        sent(PAIRF)
        pl.when(has_across)(lambda: sent(YA))
        pl.when(has_ahead & (outer | jnp.logical_not(shared(k, seam_ahead))))(lambda: sent(YB))
        pl.when(has_behind & (outer | jnp.logical_not(shared(k, seam_behind))))(lambda: sent(YBF))
        pl.when(has_across & inner & shared(k, seam_a))(lambda: sent(YP))
        pl.when(has_behind & outer & shared(k, seam_behind))(lambda: sent(YPF))
        by_relay = relay_b & (k < 0)
        for j in range(PIECES):
            by_relay = by_relay | (relay_b & (j < relays) & (k == arrival(ring_of(b_group), j)))
        pl.when(by_relay)(lambda: sent(RBF))

        @pl.when(jnp.logical_not(stays & (k // PARTS == row)))
        def _():
            sent(OUT)

        arrived(out_ref.at[k // PARTS, pl.ds((k % PARTS) * SIZE, SIZE)], OUT, k)
        return 0

    lax.fori_loop(0, PIECES, finish, 0)


def match_index(density_cols, hamilton_cols):
    start = Place().start
    left = lax.dynamic_slice_in_dim(density_cols, start, ROWS, 0)
    pairs = left.reshape(-1)
    right = jnp.take(hamilton_cols, pairs, axis=0).T
    wanted = jnp.broadcast_to(left.T[:, :, None], (LIST, ROWS, LIST)).reshape(LIST, -1)
    n = jnp.arange(1, LIST + 1, dtype=jnp.int32)[:, None, None]
    place = jnp.sum(jnp.where(right[:, None, :] == wanted[None, :, :], n, 0), axis=0)
    block = (pairs - start + W)[None, :] * LIST + place - 1
    return jnp.where(place > 0, block, WINDOW * LIST).astype(jnp.int32)


def per_device(density_blocks, hamilton_blocks, density_cols, hamilton_cols):
    index = match_index(density_cols, hamilton_cols)
    block = density_blocks.shape[2:]
    kind = density_blocks.dtype
    return pl.pallas_call(
        kernel,
        out_shape=jax.ShapeDtypeStruct(density_blocks.shape, kind),
        in_specs=[
            pl.BlockSpec(memory_space=pltpu.SMEM),
            pl.BlockSpec(memory_space=pl.ANY),
            pl.BlockSpec(memory_space=pl.ANY),
        ],
        out_specs=pl.BlockSpec(memory_space=pl.ANY),
        scratch_shapes=[
            pltpu.VMEM((WINDOW * LIST + 1, *block), kind),
            pltpu.VMEM((ROWS * LIST, *block), kind),
            pltpu.VMEM((ROWS * LIST, *block), kind),
            pltpu.VMEM((PIECES * SIZE, *block), kind),
            pltpu.SemaphoreType.DMA((13, PIECES)),
            pltpu.SemaphoreType.DMA((13, PIECES)),
        ],
        compiler_params=pltpu.CompilerParams(
            collective_id=0, has_side_effects=True, vmem_limit_bytes=52 << 20
        ),
        name="block_product",
    )(index, density_blocks, hamilton_blocks)


def solution(mesh):
    return jax.shard_map(
        per_device,
        mesh=mesh,
        in_specs=(
            P(("row", "col"), None, None, None),
            P(("row", "col"), None, None, None),
            P(),
            P(),
        ),
        out_specs=P(("row", "col"), None, None, None),
        check_vma=False,
    )
```
